128 devices in a mesh: seq: 16 (over z, y), trk: 8 (over x, core).
Axes of the slice: x: 4, y: 4, z: 4, core: 2. Of those that a mesh axis runs over, the one named last changes fastest.
Arguments:
- inputs: bfloat16 [8, 4096, 1536], P('trk', 'seq'), may hold values from -6 to 6
- layernorm_gain: float32 [1536], replicated, may hold values from 0.5 to 1.5
- dilated_weight: bfloat16 [3, 1536, 768], replicated, may hold values from -0.09375 to 0.09375
- mix_weight: bfloat16 [768, 1536], replicated, may hold values from -0.21875 to 0.21875
- head_weight: bfloat16 [1536, 4096], P(None, 'trk'), may hold values from -0.15625 to 0.15625
- head_bias: float32 [4096], P('trk'), may hold values from -1 to 1
- stored_tiles: bfloat16 [512, 4096, 128], P(('seq', 'trk')), may hold values from 0 to 4
- slot_tiles: int32 [512], replicated, may hold values from -1 to 255, as said below
Outputs:
- input_grad: float32 [8, 4096, 1536], P('trk', 'seq')
The draws below stay inside these ranges and needn't reach their ends.
Inputs may be any that keep to these rules, and one draw needn't show every extreme that they name: `slot_tiles`: slots are listed device by device in mesh order, 4 for each device. Each tile number s * 32 + k (sequence s, track block k) stands in exactly one slot; the others hold -1. Track block k belongs to group k // 4. The devices of one trk index hold together at most 8 tiles of each group, and each group has exactly 8 tiles at some trk index. Some device's slots are all used.
All inputs are finite; a program needn't handle non-finite values.
Results may differ from the reference program's by a relative error of at most 0.011.
Values may be sent and summed in bfloat16 or wider, within the bound.
No kernel may reach another device: no remote copies, remote signals or barrier semaphores. Data moves between devices by JAX's collectives and lax.ppermute only.
A program may use at most 128 MiB of HBM per device.

```python
import jax
import jax.numpy as jnp
from jax import lax

C = 1536
C2 = 768
TILE_TRACKS = 128
SPANS = 32
DILATION_STEP = 64
SEQS = 8
SEQUENCE_BINS = 4096
TRACKS = 4096
OWN_SPANS = 4
CAP = 4
N_SEQ = 16
N_TRK = 8


def draw_slot_tiles(key, part):
    key = jax.random.fold_in(key, 7)
    blocks = OWN_SPANS
    per_owner = SEQS * blocks
    n_tiles = SEQS * SPANS
    pattern = jnp.concatenate([jnp.array([2 * blocks, 0], jnp.int32), jnp.full((N_TRK - 2,), blocks, jnp.int32)])
    owner_keys = jax.random.split(jax.random.fold_in(key, 1), N_TRK)
    orders = jax.vmap(lambda k: jax.random.permutation(k, N_TRK))(owner_keys)
    counts = pattern[orders]
    edges = jnp.cumsum(counts, axis=1)
    places = jnp.arange(per_owner, dtype=jnp.int32)
    col_of_place = jnp.sum((places[None, :, None] >= edges[:, None, :]).astype(jnp.int32), axis=2)
    shuffle_keys = jax.random.split(jax.random.fold_in(key, 2), N_TRK)
    shuffles = jax.vmap(lambda k: jax.random.permutation(k, per_owner))(shuffle_keys)
    tile_col = jnp.take_along_axis(col_of_place, shuffles, axis=1)
    seq_of = places // blocks
    block_of = places % blocks
    owners = jnp.arange(N_TRK, dtype=jnp.int32)
    tile_ids = seq_of[None, :] * SPANS + owners[:, None] * blocks + block_of[None, :]
    tile_ids = tile_ids.reshape(-1).astype(jnp.int32)
    columns = tile_col.reshape(-1).astype(jnp.int32)
    priority = jax.random.permutation(jax.random.fold_in(key, 3), n_tiles).astype(jnp.int32)
    order = jnp.argsort(columns * n_tiles + priority)
    position = jnp.zeros((n_tiles,), jnp.int32).at[order].set(jnp.arange(n_tiles, dtype=jnp.int32))
    starts = jnp.sum((columns[None, :] < owners[:, None]).astype(jnp.int32), axis=1)
    within = position - starts[columns]
    device_keys = jax.random.split(jax.random.fold_in(key, 4), N_TRK)
    device_orders = jax.vmap(lambda k: jax.random.permutation(k, N_SEQ))(device_keys)
    seq_device = device_orders[columns, within // CAP]
    slot = (seq_device * N_TRK + columns) * CAP + within % CAP
    return jnp.full((N_SEQ * N_TRK * CAP,), -1, jnp.int32).at[slot].set(tile_ids)


def block_levels(rng, extent, shards, low, top_value):
    level = 1.0
    for dim, blocks in shards:
        draws = jax.random.uniform(jax.random.fold_in(jax.random.fold_in(rng, 6), dim), (blocks,), jnp.float32, low / len(shards), top_value / len(shards))
        level = level * jnp.repeat(jnp.exp(draws), extent[dim] // blocks).reshape((-1,) + (1,) * (len(extent) - 1 - dim))
    return level


def gaussian(key, dims, width, reach, cuts=(), kind=jnp.bfloat16):
    entries = width * jax.random.normal(key, dims, jnp.float32)
    if cuts:
        entries = entries * block_levels(key, dims, cuts, -0.22, 0.18)
    return jnp.clip(entries, -reach, reach).astype(kind)


def setup_inputs(seed: int = 0) -> dict:
    arg_keys = jax.random.split(jax.random.key(seed), 9)
    return {
        "inputs": gaussian(arg_keys[0], (SEQS, SEQUENCE_BINS, C), 1.0, 6.0, ((0, 8), (1, 16))),
        "layernorm_gain": jnp.clip(jax.random.uniform(arg_keys[1], (C,), jnp.float32, 0.5, 1.5), 0.5, 1.5),
        "dilated_weight": gaussian(arg_keys[2], (3, C, C2), (3 * C) ** -0.5, 0.09375),
        "mix_weight": gaussian(arg_keys[3], (C2, C), C2 ** -0.5, 0.21875),
        "head_weight": gaussian(arg_keys[4], (C, TRACKS), C ** -0.5, 0.15625, ((1, 8),)),
        "head_bias": jnp.clip(jax.random.uniform(arg_keys[5], (TRACKS,), jnp.float32, -1.0, 1.0) * block_levels(arg_keys[5], (TRACKS,), ((0, 8),), -0.4, 0.0), -1.0, 1.0),
        "stored_tiles": jnp.clip(4.0 * jax.random.uniform(arg_keys[6], (N_SEQ * N_TRK * CAP, SEQUENCE_BINS, TILE_TRACKS), jnp.float32) ** block_levels(arg_keys[6], (N_SEQ * N_TRK * CAP, SEQUENCE_BINS, TILE_TRACKS), ((0, 128),), -0.2, 0.2), 0.0, 4.0).astype(jnp.bfloat16),
        "slot_tiles": draw_slot_tiles(jax.random.fold_in(arg_keys[8], 71), 0),
    }


SQRT_HALF = 0.7071067811865476
INV_SQRT_TAU = 0.3989422804014327

def gelu_exact(v):
    return 0.5 * v * (1.0 + lax.erf(v * SQRT_HALF))

def gelu_slope(v):
    return 0.5 * (1.0 + lax.erf(v * SQRT_HALF)) + v * jnp.exp(-0.5 * v * v) * INV_SQRT_TAU

def reference(inputs, layernorm_gain, dilated_weight, mix_weight, head_weight, head_bias, stored_tiles, slot_tiles):
    n_tiles = SEQS * SPANS
    n_slots = slot_tiles.shape[0]
    safe = jnp.where(slot_tiles >= 0, slot_tiles, n_tiles).astype(jnp.int32)
    where_tile = jnp.zeros((n_tiles,), jnp.int32).at[safe].set(jnp.arange(n_slots, dtype=jnp.int32), mode='drop')
    own_tracks = TRACKS // N_TRK

    def one_sequence(args):
        x_seq, seq_index = args
        picks = lax.dynamic_slice_in_dim(where_tile, (seq_index * SPANS).astype(jnp.int32), SPANS)
        tiles = jnp.take(stored_tiles, picks, axis=0)
        target = tiles.transpose(1, 0, 2).reshape(SEQUENCE_BINS, TRACKS).astype(jnp.float32)
        x_rows = x_seq.astype(jnp.float32)
        centre_offset = x_rows - lax.optimization_barrier(jnp.mean(x_rows, axis=1, keepdims=True))
        inverse_deviation = lax.rsqrt(lax.optimization_barrier(jnp.mean(centre_offset * centre_offset, axis=1, keepdims=True)) + 1e-05)
        centred_normalized = centre_offset * inverse_deviation
        normalized_rows = centred_normalized * layernorm_gain
        activated_rows = gelu_exact(normalized_rows).astype(jnp.bfloat16)
        padded_input = jnp.pad(activated_rows, ((DILATION_STEP, DILATION_STEP), (0, 0)))
        preactivation = jnp.zeros((SEQUENCE_BINS, C2), jnp.float32)
        for tap_number in range(3):
            preactivation = preactivation + jnp.dot(padded_input[tap_number * DILATION_STEP:tap_number * DILATION_STEP + SEQUENCE_BINS], dilated_weight[tap_number], preferred_element_type=jnp.float32)
        inner = gelu_exact(preactivation).astype(jnp.bfloat16)
        embed = (x_rows + jnp.dot(inner, mix_weight, preferred_element_type=jnp.float32)).astype(jnp.bfloat16)
        logits = jnp.dot(embed, head_weight, preferred_element_type=jnp.float32) + head_bias
        pred = jax.nn.softplus(logits)
        d_logits = ((1.0 - target / pred) * jax.nn.sigmoid(logits)).astype(jnp.bfloat16)
        grouped_rows = d_logits.reshape(SEQUENCE_BINS, N_TRK, own_tracks).astype(jnp.float32)
        head_partitions = head_weight.reshape(C, N_TRK, own_tracks).astype(jnp.float32)
        partial_pieces = jnp.einsum('qnp,enp->nqe', grouped_rows, head_partitions).astype(jnp.bfloat16)
        d_embed = lax.optimization_barrier(jnp.sum(partial_pieces, axis=0, dtype=jnp.float32))
        d_half = d_embed.astype(jnp.bfloat16)
        d_inner = jnp.dot(d_half, mix_weight.T, preferred_element_type=jnp.float32)
        preact_gradient = (d_inner * gelu_slope(preactivation)).astype(jnp.bfloat16)
        padded_gradient = jnp.pad(preact_gradient, ((DILATION_STEP, DILATION_STEP), (0, 0)))
        d_act = jnp.zeros((SEQUENCE_BINS, C), jnp.float32)
        for tap_number in range(3):
            start_offset = (2 - tap_number) * DILATION_STEP
            d_act = d_act + jnp.dot(padded_gradient[start_offset:start_offset + SEQUENCE_BINS], dilated_weight[tap_number].T, preferred_element_type=jnp.float32)
        scaled_rows = d_act * gelu_slope(normalized_rows) * layernorm_gain
        backward_fn = scaled_rows - lax.optimization_barrier(jnp.mean(scaled_rows, axis=1, keepdims=True)) - centred_normalized * lax.optimization_barrier(jnp.mean(scaled_rows * centred_normalized, axis=1, keepdims=True))
        return d_embed + inverse_deviation * backward_fn
    return lax.map(one_sequence, (inputs, jnp.arange(SEQS, dtype=jnp.int32)))
```

```python
import jax
import jax.numpy as jnp
import numpy as np
from jax import lax
from jax.sharding import PartitionSpec as P

DILATION_STEP = 64
ROOM = 24

SQRT_HALF = 0.7071067811865476
INV_SQRT_TAU = 0.3989422804014327

SEQ = ("z", "y")
TRK = ("x", "core")


def halo(value, width):
    size = lax.axis_size(SEQ)
    up = [(i, i + 1) for i in range(size - 1)]
    down = [(j, i) for i, j in up]
    before = lax.ppermute(value[value.shape[0] - width :], SEQ, up)
    after = lax.ppermute(value[:width], SEQ, down)
    return before, after


def gelu_exact(v):
    return 0.5 * v * (1.0 + lax.erf(v * SQRT_HALF))


def gelu_slope(v):
    return 0.5 * (1.0 + lax.erf(v * SQRT_HALF)) + v * jnp.exp(-0.5 * v * v) * INV_SQRT_TAU


def core_swap(value):
    return lax.ppermute(value, "core", [(0, 1), (1, 0)])


def shards(
    inputs,
    layernorm_gain,
    dilated_weight,
    mix_weight,
    head_weight,
    head_bias,
    stored_tiles,
    slot_tiles,
):
    n_q = lax.axis_size(SEQ)
    n_x = lax.axis_size("x")
    n_c = lax.axis_size("core")
    x_index = lax.axis_index("x")
    core = lax.axis_index("core")
    bins, width = inputs.shape[1:]
    half = bins // n_c
    tracks = head_weight.shape[1] * n_x * n_c
    slots, _, tile = stored_tiles.shape
    spans = tracks // tile
    depth = n_q * n_c * slots
    want = n_c * spans

    full_head = lax.all_gather(head_weight, TRK, axis=1, tiled=True)
    full_bias = lax.all_gather(head_bias, TRK, axis=0, tiled=True)

    outbound = (
        stored_tiles.reshape(slots, n_q, n_c, half, tile)
        .transpose(1, 2, 0, 3, 4)
        .reshape(depth, half, tile)
    )
    pieces = lax.all_to_all(outbound, ("z", "y", "core"), 0, 0, tiled=True)

    table = slot_tiles.reshape(n_q, n_x, n_c * slots).transpose(1, 0, 2).reshape(n_x, depth)
    dest = jnp.where(table >= 0, table // want, n_x)
    chips = jnp.arange(n_x, dtype=jnp.int32)
    marks = dest[:, :, None] == chips[None, None, :]
    place = jnp.arange(depth, dtype=jnp.int32)
    same = dest[:, :, None] == dest[:, None, :]
    rank = jnp.sum(same & (place[None, None, :] < place[None, :, None]), axis=2, dtype=jnp.int32)
    fullest = jnp.max(jnp.sum(marks, axis=1, dtype=jnp.int32))
    my_dest = lax.dynamic_index_in_dim(dest, x_index, 0, keepdims=False)
    my_rank = lax.dynamic_index_in_dim(rank, x_index, 0, keepdims=False)

    def source(first, count):
        order = first + jnp.arange(count, dtype=jnp.int32)
        hit = (my_dest[None, None, :] == chips[:, None, None]) & (
            my_rank[None, None, :] == order[None, :, None]
        )
        return jnp.sum(hit * place, axis=2, dtype=jnp.int32).reshape(-1)

    sent = jnp.take(pieces, source(0, ROOM), axis=0, mode="clip")
    arrived = lax.all_to_all(sent, "x", 0, 0, tiled=True)

    tiles_wanted = (
        (x_index * n_c + jnp.stack([core, 1 - core]))[:, None] * spans
        + jnp.arange(spans, dtype=jnp.int32)[None, :]
    ).reshape(-1)
    found = tiles_wanted[:, None, None] == table[None]
    came = jnp.where(
        rank < ROOM,
        chips[:, None] * ROOM + rank,
        n_x * ROOM + chips[:, None] * (want - ROOM) + rank - ROOM,
    )
    where = jnp.sum(found * came[None], axis=(1, 2), dtype=jnp.int32)

    def roomy(arrived, pieces, where):
        return jnp.take(arrived, where, axis=0, mode="clip")

    def crowded(arrived, pieces, where):
        more = jnp.take(pieces, source(ROOM, want - ROOM), axis=0, mode="clip")
        rest = lax.all_to_all(more, "x", 0, 0, tiled=True)
        return jnp.take(jnp.concatenate([arrived, rest]), where, axis=0, mode="clip")

    target = lax.cond(fullest > ROOM, crowded, roomy, arrived, pieces, where)
    target = target.reshape(n_c, spans, half, tile).transpose(0, 2, 1, 3).reshape(bins, tracks)

    x_rows = inputs[0].astype(jnp.float32)
    centre_offset = x_rows - jnp.mean(x_rows, axis=1, keepdims=True)
    inverse_deviation = lax.rsqrt(
        jnp.mean(centre_offset * centre_offset, axis=1, keepdims=True) + 1e-05
    )
    centred_normalized = centre_offset * inverse_deviation
    normalized_rows = centred_normalized * layernorm_gain
    activated_rows = gelu_exact(normalized_rows).astype(jnp.bfloat16)
    before, after = halo(activated_rows, DILATION_STEP)
    padded_input = jnp.concatenate([before, activated_rows, after])
    preactivation = jnp.zeros((bins, dilated_weight.shape[2]), jnp.float32)
    for tap in range(3):
        preactivation = preactivation + jnp.dot(
            padded_input[tap * DILATION_STEP : tap * DILATION_STEP + bins],
            dilated_weight[tap],
            preferred_element_type=jnp.float32,
        )
    inner = gelu_exact(preactivation).astype(jnp.bfloat16)
    embed = (x_rows + jnp.dot(inner, mix_weight, preferred_element_type=jnp.float32)).astype(
        jnp.bfloat16
    )
    halves = embed.reshape(n_c, half, width)
    mine = lax.dynamic_index_in_dim(halves, core, 0, keepdims=False)
    theirs = lax.dynamic_index_in_dim(halves, 1 - core, 0, keepdims=False)
    rows = jnp.concatenate([mine, core_swap(theirs)])

    logits = jnp.dot(rows, full_head, preferred_element_type=jnp.float32) + full_bias
    pred = jax.nn.softplus(logits)
    d_logits = ((1.0 - target.astype(jnp.float32) / pred) * jax.nn.sigmoid(logits)).astype(
        jnp.bfloat16
    )
    d_rows = lax.dot_general(
        d_logits, full_head, (((1,), (1,)), ((), ())), preferred_element_type=jnp.float32
    )
    kept = d_rows[:half]
    back = core_swap(d_rows[half:])
    d_embed = jnp.where(
        core == 0, jnp.concatenate([kept, back]), jnp.concatenate([back, kept])
    )
    d_half = d_embed.astype(jnp.bfloat16)
    d_inner = lax.dot_general(
        d_half, mix_weight, (((1,), (1,)), ((), ())), preferred_element_type=jnp.float32
    )
    preact_gradient = (d_inner * gelu_slope(preactivation)).astype(jnp.bfloat16)
    before, after = halo(preact_gradient, DILATION_STEP)
    padded_gradient = jnp.concatenate([before, preact_gradient, after])
    d_act = jnp.zeros((bins, width), jnp.float32)
    for tap in range(3):
        start = (2 - tap) * DILATION_STEP
        d_act = d_act + lax.dot_general(
            padded_gradient[start : start + bins],
            dilated_weight[tap],
            (((1,), (1,)), ((), ())),
            preferred_element_type=jnp.float32,
        )
    scaled_rows = d_act * gelu_slope(normalized_rows) * layernorm_gain
    backward_fn = (
        scaled_rows
        - jnp.mean(scaled_rows, axis=1, keepdims=True)
        - centred_normalized * jnp.mean(scaled_rows * centred_normalized, axis=1, keepdims=True)
    )
    return (d_embed + inverse_deviation * backward_fn)[None]


def solution(mesh):
    chips = jax.sharding.Mesh(
        np.asarray(mesh.devices).reshape(4, 4, 4, 2), ("z", "y", "x", "core")
    )
    in_specs = (
        P(TRK, SEQ, None),
        P(),
        P(),
        P(),
        P(None, TRK),
        P(TRK),
        P(SEQ + TRK, None, None),
        P(),
    )
    out_specs = P(TRK, SEQ, None)
    return jax.shard_map(
        shards, mesh=chips, in_specs=in_specs, out_specs=out_specs, check_vma=False
    )
```

```python
import jax
import jax.numpy as jnp
import numpy as np
from jax import lax
from jax.experimental import pallas as pl
from jax.experimental.pallas import tpu as pltpu
from jax.sharding import PartitionSpec as P

DILATION_STEP = 64
ROOM = 24
SPARE = 8
LEAD = 12

SQRT_HALF = 0.7071067811865476
INV_SQRT_TAU = 0.3989422804014327

SEQ = ("z", "y")
TRK = ("x", "core")


def halo(last, first):
    size = lax.axis_size(SEQ)
    up = [(i, i + 1) for i in range(size - 1)]
    down = [(j, i) for i, j in up]
    return lax.ppermute(last, SEQ, up), lax.ppermute(first, SEQ, down)


def core_swap(value):
    return lax.ppermute(value, "core", [(0, 1), (1, 0)])


ANY = pl.BlockSpec(memory_space=pl.ANY)
FREE = pl.CostEstimate(flops=0, bytes_accessed=0, transcendentals=0)


def room(mib):
    return pltpu.CompilerParams(vmem_limit_bytes=mib * 1024 * 1024)


def nt_dot(a, b):
    return lax.dot_general(a, b, (((1,), (1,)), ((), ())), preferred_element_type=jnp.float32)


def arrange(stored, parts, after):
    slots, bins, tile = stored.shape
    each = bins // parts

    def kernel(in_ref, *rest):
        out_ref, held, into, out = rest[len(after) :]
        reads = [pltpu.make_async_copy(in_ref.at[s], held.at[s], into.at[s]) for s in range(slots)]
        writes = [
            pltpu.make_async_copy(held.at[s], out_ref.at[:, s], out.at[s]) for s in range(slots)
        ]
        for read in reads:
            read.start()
        for read, write in zip(reads, writes):
            read.wait()
            write.start()
        for write in writes:
            write.wait()

    return pl.pallas_call(
        kernel,
        out_shape=jax.ShapeDtypeStruct((parts, slots, each, tile), stored.dtype),
        in_specs=[ANY] * (1 + len(after)),
        out_specs=ANY,
        scratch_shapes=[
            pltpu.VMEM((slots, parts, each, tile), stored.dtype),
            pltpu.SemaphoreType.DMA((slots,)),
            pltpu.SemaphoreType.DMA((slots,)),
        ],
        compiler_params=room(56),
        cost_estimate=FREE,
    )(stored.reshape(slots, parts, each, tile), *after)


def head_block(head, bias, extra):
    width, own = head.shape
    full = pl.BlockSpec(memory_space=pltpu.VMEM)

    def kernel(head_ref, bias_ref, out_ref):
        out_ref[:own] = head_ref[...].T
        out_ref[own:] = jnp.zeros((extra, width), head.dtype)
        left = bias_ref[...]
        for part in range(width // own):
            piece = left.astype(jnp.bfloat16)
            left = left - piece.astype(jnp.float32)
            out_ref[own : own + 1, part * own : (part + 1) * own] = piece

    return pl.pallas_call(
        kernel,
        out_shape=jax.ShapeDtypeStruct((own + extra, width), head.dtype),
        in_specs=[full, full],
        out_specs=full,
        compiler_params=room(16),
        cost_estimate=FREE,
    )(head, bias[None])


def norm_pass(before, x, after, gain):
    bins, width = x.shape
    step = before.shape[0]
    full = pl.BlockSpec(memory_space=pltpu.VMEM)

    def kernel(before_ref, x_ref, after_ref, gain_ref, out_ref, xhat_ref, factor_ref, scale_ref):
        chunks = [(before_ref, 0)] + [(x_ref, i) for i in range(0, bins, step)] + [(after_ref, 0)]
        for i, (ref, top) in enumerate(chunks):
            rows = ref[pl.ds(top, step)].astype(jnp.float32)
            offset = rows - jnp.mean(rows, axis=1, keepdims=True)
            scale = lax.rsqrt(jnp.mean(offset * offset, axis=1, keepdims=True) + 1e-05)
            xhat = offset * scale
            v = xhat * gain_ref[...]
            phi = 0.5 * (1.0 + lax.erf(v * SQRT_HALF))
            out_ref[pl.ds(i * step, step)] = (v * phi).astype(jnp.bfloat16)
            if ref is x_ref:
                at = pl.ds(top, step)
                slope = phi + v * jnp.exp(-0.5 * v * v) * INV_SQRT_TAU
                xhat_ref[at] = xhat
                factor_ref[at] = slope * gain_ref[...]
                scale_ref[at] = scale

    wide = jax.ShapeDtypeStruct((bins, width), jnp.float32)
    return pl.pallas_call(
        kernel,
        out_shape=(
            jax.ShapeDtypeStruct((bins + 2 * step, width), jnp.bfloat16),
            wide,
            wide,
            jax.ShapeDtypeStruct((bins, 1), jnp.float32),
        ),
        in_specs=[full] * 4,
        out_specs=(full,) * 4,
        compiler_params=room(12),
        cost_estimate=FREE,
    )(before, x, after, gain[None])


def blank(shape, dtype):
    return pl.pallas_call(
        lambda out_ref: None,
        out_shape=jax.ShapeDtypeStruct(shape, dtype),
        out_specs=ANY,
        cost_estimate=FREE,
    )()


def pick_kernel(count, index_ref, pieces_ref, out_ref, mark_ref, sem):
    def start(i, carry):
        pltpu.make_async_copy(pieces_ref.at[index_ref[i]], out_ref.at[i], sem).start()
        return carry

    lax.fori_loop(0, count, start, 0, unroll=8)
    mark_ref[...] = jnp.zeros_like(mark_ref)
    pltpu.make_async_copy(pieces_ref.at[pl.ds(0, count)], out_ref, sem).wait()


def pick(pieces, index):
    count = index.shape[0]
    block = (count,) + pieces.shape[1:]
    return pl.pallas_call(
        lambda *refs: pick_kernel(count, *refs),
        out_shape=(
            jax.ShapeDtypeStruct(block, pieces.dtype),
            jax.ShapeDtypeStruct((8, 128), jnp.float32),
        ),
        grid_spec=pltpu.PrefetchScalarGridSpec(
            num_scalar_prefetch=1,
            grid=(1,),
            in_specs=[ANY],
            out_specs=(
                pl.BlockSpec(block, lambda i, index: (0, 0, 0)),
                pl.BlockSpec((8, 128), lambda i, index: (0, 0)),
            ),
            scratch_shapes=[pltpu.SemaphoreType.DMA],
        ),
        compiler_params=room(16),
        cost_estimate=FREE,
    )(index, pieces)


def gate(value, *others, lead=0):
    return pl.pallas_call(
        lambda *refs: None,
        out_shape=jax.ShapeDtypeStruct(value.shape, value.dtype),
        in_specs=[ANY] * (1 + len(others)),
        out_specs=ANY,
        input_output_aliases={0: 0},
        cost_estimate=pl.CostEstimate(flops=lead * 10**9, bytes_accessed=0, transcendentals=0),
    )(value, *others)


def fetch(g, blocks, held, sems, go):
    for j, parts in enumerate(blocks):

        @pl.when(g == j)
        def _():
            top = 0
            for part in parts:
                copy = pltpu.make_async_copy(
                    part, held.at[j % 2, pl.ds(top, part.shape[0])], sems.at[j % 2]
                )
                copy.start() if go else copy.wait()
                top += part.shape[0]


def next_block(g, blocks, held, sems):
    @pl.when(g == 0)
    def _():
        fetch(g, blocks, held, sems, True)

    fetch(g, blocks, held, sems, False)
    fetch(g + 1, blocks, held, sems, True)


def nest(flat, counts):
    out = []
    for n in counts:
        out.append(flat[:n])
        flat = flat[n:]
    return out


def forward_kernel(core_ref, act_ref, x_ref, taps_ref, mix_ref, *rest):
    slope_ref, mine_ref, theirs_ref, mark_ref, embed = rest
    mark_ref[...] = jnp.zeros_like(mark_ref)
    bins = x_ref.shape[0]
    step = (act_ref.shape[0] - bins) // 2
    half = mine_ref.shape[0]

    def dot(a, b):
        return jnp.dot(a, b, preferred_element_type=jnp.float32)

    v = dot(act_ref[:bins], taps_ref[0])
    v = v + dot(act_ref[step : step + bins], taps_ref[1])
    v = v + dot(act_ref[2 * step :], taps_ref[2])
    phi = 0.5 * (1.0 + lax.erf(v * SQRT_HALF))
    slope_ref[...] = phi + v * jnp.exp(-0.5 * v * v) * INV_SQRT_TAU
    embed[...] = x_ref[...].astype(jnp.float32) + dot((v * phi).astype(jnp.bfloat16), mix_ref[...])
    at = pl.multiple_of(core_ref[0] * half, half)
    mine_ref[...] = embed[pl.ds(at, half)].astype(jnp.bfloat16)
    theirs_ref[...] = embed[pl.ds(half - at, half)].astype(jnp.bfloat16)


def forward_pass(core, act, x, taps, mix, half):
    bins, width = x.shape
    inner = taps.shape[2]
    out = jax.ShapeDtypeStruct((half, width), jnp.bfloat16)
    full = pl.BlockSpec(memory_space=pltpu.VMEM)
    return pl.pallas_call(
        forward_kernel,
        out_shape=(
            jax.ShapeDtypeStruct((bins, inner), jnp.float32),
            out,
            out,
            jax.ShapeDtypeStruct((8, 128), jnp.float32),
        ),
        in_specs=[pl.BlockSpec(memory_space=pltpu.SMEM)] + [full] * 4,
        out_specs=(full,) * 4,
        scratch_shapes=[pltpu.VMEM((bins, width), jnp.float32)],
        compiler_params=room(18),
        cost_estimate=FREE,
    )(core, act, x, taps, mix)


def head_kernel(counts, own, mine_ref, other_ref, *rest):
    sig_ref, ratio_ref, head_ref, rows, held, sems = rest[-6:]
    g = pl.program_id(0)
    half = mine_ref.shape[0]

    @pl.when(g == 0)
    def _():
        rows[:half] = mine_ref[...]
        rows[half:] = other_ref[...]

    next_block(g, nest(rest[: sum(counts)], counts), held, sems)
    w = held.at[g % 2]
    head_ref[...] = w[:own]
    logits = nt_dot(rows[...], w[:own])
    bias = jnp.sum(w[own:].astype(jnp.float32), axis=0, keepdims=True)
    for part in range(bias.shape[1] // own):
        logits = logits + bias[:, part * own : (part + 1) * own]
    e = jnp.exp(-jnp.abs(logits))
    inverse = 1.0 / (1.0 + e)
    sig = jnp.where(logits >= 0.0, inverse, e * inverse)
    pred = jnp.maximum(logits, 0.0) + jnp.log1p(e)
    sig_ref[...] = sig
    ratio_ref[...] = sig / pred


def head_pass(mine, other, blocks, own, others):
    half, width = mine.shape
    n = 2 * half
    counts = [len(parts) for parts in blocks]
    flat = [part for parts in blocks for part in parts]
    tall = blocks[0][0].shape[0]
    tracks = own * len(blocks)
    out = jax.ShapeDtypeStruct((n, tracks), jnp.float32)
    out_spec = pl.BlockSpec((n, own), lambda g: (0, g))
    row_spec = pl.BlockSpec((half, width), lambda g: (0, 0))
    return pl.pallas_call(
        lambda *refs: head_kernel(counts, own, *refs),
        out_shape=(out, out, jax.ShapeDtypeStruct((tracks, width), mine.dtype)),
        grid=(len(blocks),),
        in_specs=[row_spec, row_spec] + [ANY] * (len(flat) + len(others)),
        out_specs=(out_spec, out_spec, pl.BlockSpec((own, width), lambda g: (g, 0))),
        scratch_shapes=[
            pltpu.VMEM((n, width), jnp.bfloat16),
            pltpu.VMEM((2, tall, width), jnp.bfloat16),
            pltpu.SemaphoreType.DMA((2,)),
        ],
        compiler_params=room(14),
        cost_estimate=FREE,
    )(mine, other, *flat, *others)


def grad_kernel(kinds, own_spans, plan_ref, sig_ref, ratio_ref, *rest):
    sources = rest[:kinds]
    kept_ref, sent_ref, tiles, sems = rest[kinds:]
    half, tile = tiles.shape[1:]
    spans = sig_ref.shape[1] // tile
    per = 2 * own_spans
    usual = kinds // 2 + 1

    def copies(group, go):
        top = sum(source.shape[0] for source in sources[: group[0]])
        for k in group:
            copy = pltpu.make_async_copy(
                sources[k], tiles.at[pl.ds(top, sources[k].shape[0])], sems.at[k]
            )
            copy.start() if go else copy.wait()
            top += sources[k].shape[0]

    copies(range(usual), True)

    @pl.when(plan_ref[2 * spans] > 0)
    def _():
        copies(range(usual, kinds), True)
        copies(range(usual, kinds), False)

    copies(range(usual), False)
    for s, out_ref in enumerate((kept_ref, sent_ref)):
        for k in range(spans):
            cols = pl.ds(k * tile, tile)
            at = (pl.ds(s * half, half), cols)
            spot = plan_ref[k // own_spans * per + s * own_spans + k % own_spans]
            t = tiles[spot].astype(jnp.float32)
            out_ref[:, cols] = (sig_ref[at] - t * ratio_ref[at]).astype(jnp.bfloat16)


def grad_pass(plan, sig, ratio, sources, own_spans):
    n, tracks = sig.shape
    half, tile = sources[0].shape[1:]
    out = jax.ShapeDtypeStruct((half, tracks), jnp.bfloat16)
    full = pl.BlockSpec(memory_space=pltpu.VMEM)
    total = sum(source.shape[0] for source in sources)
    return pl.pallas_call(
        lambda *refs: grad_kernel(len(sources), own_spans, *refs),
        out_shape=(out, out),
        in_specs=[pl.BlockSpec(memory_space=pltpu.SMEM), full, full] + [ANY] * len(sources),
        out_specs=(full, full),
        scratch_shapes=[
            pltpu.VMEM((total, half, tile), jnp.bfloat16),
            pltpu.SemaphoreType.DMA((len(sources),)),
        ],
        compiler_params=room(12),
        cost_estimate=FREE,
    )(plan, sig, ratio, *sources)


def inner_pass(core, kept, back, mix, slope, step):
    half, width = kept.shape
    bins, inner = slope.shape
    full = pl.BlockSpec(memory_space=pltpu.VMEM)

    def kernel(core_ref, kept_ref, back_ref, mix_ref, slope_ref, embed_ref, pre_ref, *ends):
        at = pl.multiple_of(core_ref[0] * half, half)
        embed_ref[pl.ds(at, half)] = kept_ref[...]
        embed_ref[pl.ds(half - at, half)] = back_ref[...]
        d_inner = nt_dot(embed_ref[...].astype(jnp.bfloat16), mix_ref[...])
        d_pre = (d_inner * slope_ref[...]).astype(jnp.bfloat16)
        pre_ref[...] = d_pre
        ends[0][...] = d_pre[:step]
        ends[1][...] = d_pre[bins - step :]

    end = jax.ShapeDtypeStruct((step, inner), jnp.bfloat16)
    return pl.pallas_call(
        kernel,
        out_shape=(
            jax.ShapeDtypeStruct((bins, width), jnp.float32),
            jax.ShapeDtypeStruct((bins, inner), jnp.bfloat16),
            end,
            end,
        ),
        in_specs=[pl.BlockSpec(memory_space=pltpu.SMEM)] + [full] * 4,
        out_specs=(full,) * 4,
        compiler_params=room(10),
    )(core, kept, back, mix, slope)


def local_pass(d_pre, taps, step):
    bins = d_pre.shape[0]
    width = taps.shape[1]
    full = pl.BlockSpec(memory_space=pltpu.VMEM)

    def kernel(pre_ref, taps_ref, out_ref):
        out_ref[...] = nt_dot(pre_ref[...], taps_ref[1])
        out_ref[: bins - step] += nt_dot(pre_ref[step:], taps_ref[0])
        out_ref[step:] += nt_dot(pre_ref[: bins - step], taps_ref[2])

    return pl.pallas_call(
        kernel,
        out_shape=jax.ShapeDtypeStruct((bins, width), jnp.float32),
        in_specs=[full] * 2,
        out_specs=full,
        compiler_params=room(12),
    )(d_pre, taps)


def last_pass(before, after, d_act, taps, factor, xhat, inverse, d_embed):
    step = before.shape[0]
    bins, width = d_act.shape
    full = pl.BlockSpec(memory_space=pltpu.VMEM)

    def kernel(before_ref, after_ref, act_ref, first_ref, last_ref, *rest):
        factor_ref, xhat_ref, inverse_ref, embed_ref, out_ref = rest
        head = nt_dot(before_ref[...], last_ref[0])
        tail = nt_dot(after_ref[...], first_ref[0])
        for top in range(0, bins, step):
            at = pl.ds(top, step)
            d = act_ref[at]
            if top == 0:
                d = d + head
            if top == bins - step:
                d = d + tail
            d = d * factor_ref[at]
            xhat = xhat_ref[at]
            middle = jnp.mean(d, axis=1, keepdims=True)
            slant = jnp.mean(d * xhat, axis=1, keepdims=True)
            out_ref[at] = embed_ref[at] + inverse_ref[at] * (d - middle - xhat * slant)

    def tap(i):
        return pl.BlockSpec((1,) + taps.shape[1:], lambda j: (i, 0, 0))

    return pl.pallas_call(
        kernel,
        out_shape=jax.ShapeDtypeStruct((bins, width), jnp.float32),
        grid=(1,),
        in_specs=[full] * 3 + [tap(0), tap(2)] + [full] * 4,
        out_specs=full,
        compiler_params=room(16),
    )(before, after, d_act, taps, taps, factor, xhat, inverse, d_embed)


def shards(
    inputs,
    layernorm_gain,
    dilated_weight,
    mix_weight,
    head_weight,
    head_bias,
    stored_tiles,
    slot_tiles,
):
    n_q = lax.axis_size(SEQ)
    n_x = lax.axis_size("x")
    n_c = lax.axis_size("core")
    x_index = lax.axis_index("x")
    core = lax.axis_index("core")
    bins, width = inputs.shape[1:]
    half = bins // n_c
    tracks = head_weight.shape[1] * n_x * n_c
    slots, _, tile = stored_tiles.shape
    spans = tracks // tile
    depth = n_q * n_c * slots
    want = n_c * spans
    own_tracks = head_weight.shape[1]
    own_spans = own_tracks // tile

    def step(value, shift):
        return lax.ppermute(value, "x", [(i, (i + shift) % n_x) for i in range(n_x)])

    before, after = halo(inputs[0, bins - DILATION_STEP :], inputs[0, :DILATION_STEP])
    block = head_block(head_weight, head_bias, 16)
    outbound = gate(arrange(stored_tiles, n_q * n_c, (block,)), before, after)
    pieces = lax.all_to_all(
        outbound.reshape(depth, half, tile), ("z", "y", "core"), 0, 0, tiled=True
    )
    near = [step(block, 1), step(block, -1)]
    block_x = (x_index + jnp.array([0, 0, -1, -1, 1, 1, 2, 2], jnp.int32)) % n_x
    block_c = (core + jnp.array([0, 1, 0, 1, 0, 1, 0, 1], jnp.int32)) % n_c
    group_of = block_x * n_c + block_c

    table = slot_tiles.reshape(n_q, n_x, n_c * slots).transpose(1, 0, 2).reshape(n_x, depth)
    dest = jnp.where(table >= 0, table // want, n_x)
    chips = jnp.arange(n_x, dtype=jnp.int32)
    marks = dest[:, :, None] == chips[None, None, :]
    place = jnp.arange(depth, dtype=jnp.int32)
    same = dest[:, :, None] == dest[:, None, :]
    rank = jnp.sum(same & (place[None, None, :] < place[None, :, None]), axis=2, dtype=jnp.int32)
    sizes = jnp.sum(marks, axis=1, dtype=jnp.int32)
    fullest = jnp.max(jnp.where(chips[:, None] == chips[None, :], 0, sizes))
    my_dest = lax.dynamic_index_in_dim(dest, x_index, 0, keepdims=False)
    my_rank = lax.dynamic_index_in_dim(rank, x_index, 0, keepdims=False)
    shifted = (my_dest - x_index) % n_x
    shifted = jnp.where(my_dest < n_x, shifted, n_x)
    order = jnp.arange(want, dtype=jnp.int32)
    hit = (shifted[None, None, :] == chips[:, None, None]) & (
        my_rank[None, None, :] == order[None, :, None]
    )
    outgoing = jnp.sum(hit * place, axis=2, dtype=jnp.int32)

    spots = jnp.arange(want, dtype=jnp.int32)
    spot_side = spots // own_spans % n_c
    spot_span = (
        jnp.repeat(group_of, n_c * own_spans, total_repeat_length=want) * own_spans
        + spots % own_spans
    )
    tiles_wanted = (x_index * n_c + (core + spot_side) % n_c) * spans + spot_span
    turn = ((x_index - chips) % n_x)[:, None]
    spill = want - ROOM
    usual = want + (turn - 1) * ROOM + rank
    rare = want + (n_x - 1) * ROOM + (turn - 1) * spill + rank - ROOM
    spot_in = jnp.where(turn == 0, rank, jnp.where(rank < ROOM, usual, rare))
    found = tiles_wanted[:, None, None] == table[None]
    plan = jnp.sum(found * spot_in[None], axis=(1, 2), dtype=jnp.int32)
    plan = jnp.concatenate([plan, (fullest > ROOM).astype(jnp.int32)[None]])

    core_at = core.astype(jnp.int32)[None]
    act, xhat, factor, scale = norm_pass(before, inputs[0], after, layernorm_gain)
    cut = own_tracks // 2
    far = [
        step(gate(near[0][:cut], plan, scale), 1),
        step(gate(near[1][cut:], plan, scale), -1),
    ]
    slope, mine, theirs, mark = forward_pass(
        core_at, act, inputs[0], dilated_weight, mix_weight, half
    )
    blocks = []
    for parts in ([block], [near[0]], [near[1]]):
        blocks += [parts, [core_swap(part) for part in parts]]
    blocks += [far, [core_swap(gate(part, mark)) for part in far]]
    other = core_swap(theirs)

    outgoing = gate(outgoing, plan, other, *blocks[-1], lead=LEAD)
    picked = {d: pick(pieces, outgoing[d, :ROOM])[0] for d in (2, 1, 3)}
    sent = {d: step(picked[d], d) for d in (2, 1, 3)}
    arrived = [sent[d] for d in range(1, n_x)]

    def extra(first, last):
        def send(pieces, outgoing):
            out = []
            for d in range(1, n_x):
                v = step(pick(pieces, outgoing[d, first:last])[0], d)
                out.append(jnp.pad(v, ((0, want - last), (0, 0), (0, 0))))
            return tuple(out)

        return send

    def roomy(pieces, outgoing):
        shape = (want - ROOM,) + pieces.shape[1:]
        return tuple(blank(shape, pieces.dtype) for _ in range(n_x - 1))

    level = (fullest > ROOM).astype(jnp.int32) + (fullest > ROOM + SPARE)
    more = lax.switch(
        level,
        [roomy, extra(ROOM, ROOM + SPARE), extra(ROOM, want)],
        pieces,
        outgoing,
    )
    local, _ = pick(pieces, outgoing[0])
    sig, ratio, full_head = head_pass(mine, other, blocks, own_tracks, [local] + list(more))
    d_mine, d_theirs = grad_pass(plan, sig, ratio, [local] + arrived + list(more), own_spans)
    leaving = jnp.dot(d_theirs, full_head, preferred_element_type=jnp.float32)
    kept = jnp.dot(d_mine, full_head, preferred_element_type=jnp.float32)
    d_embed, d_pre, first, last = inner_pass(
        core_at, kept, core_swap(leaving), mix_weight, slope, DILATION_STEP
    )
    before, after = halo(last, first)
    d_act = local_pass(d_pre, dilated_weight, DILATION_STEP)
    grad = last_pass(before, after, d_act, dilated_weight, factor, xhat, scale, d_embed)
    return grad[None]


def solution(mesh):
    chips = jax.sharding.Mesh(
        np.asarray(mesh.devices).reshape(4, 4, 4, 2), ("z", "y", "x", "core")
    )
    in_specs = (
        P(TRK, SEQ, None),
        P(),
        P(),
        P(),
        P(None, TRK),
        P(TRK),
        P(SEQ + TRK, None, None),
        P(),
    )
    out_specs = P(TRK, SEQ, None)
    return jax.shard_map(
        shards, mesh=chips, in_specs=in_specs, out_specs=out_specs, check_vma=False
    )
```

```python
import jax
import jax.numpy as jnp
import numpy as np
from jax import lax
from jax.experimental import pallas as pl
from jax.experimental.pallas import tpu as pltpu
from jax.sharding import PartitionSpec as P

DILATION_STEP = 64
ROOM = 24
SPARE = 4
LEAD = 12

SQRT_HALF = 0.7071067811865476
INV_SQRT_TAU = 0.3989422804014327

SEQ = ("z", "y")
TRK = ("x", "core")


def halo(last, first):
    size = lax.axis_size(SEQ)
    up = [(i, i + 1) for i in range(size - 1)]
    down = [(j, i) for i, j in up]
    return lax.ppermute(last, SEQ, up), lax.ppermute(first, SEQ, down)


def core_swap(value):
    return lax.ppermute(value, "core", [(0, 1), (1, 0)])


ANY = pl.BlockSpec(memory_space=pl.ANY)
FREE = pl.CostEstimate(flops=0, bytes_accessed=0, transcendentals=0)


def room(mib):
    return pltpu.CompilerParams(vmem_limit_bytes=mib * 1024 * 1024)


def nt_dot(a, b):
    return lax.dot_general(a, b, (((1,), (1,)), ((), ())), preferred_element_type=jnp.float32)


def arrange(stored, parts, after):
    slots, bins, tile = stored.shape
    each = bins // parts

    def kernel(in_ref, *rest):
        out_ref, held, into, out = rest[len(after) :]
        reads = [pltpu.make_async_copy(in_ref.at[s], held.at[s], into.at[s]) for s in range(slots)]
        writes = [
            pltpu.make_async_copy(held.at[s], out_ref.at[:, s], out.at[s]) for s in range(slots)
        ]
        for read in reads:
            read.start()
        for read, write in zip(reads, writes):
            read.wait()
            write.start()
        for write in writes:
            write.wait()

    return pl.pallas_call(
        kernel,
        out_shape=jax.ShapeDtypeStruct((parts, slots, each, tile), stored.dtype),
        in_specs=[ANY] * (1 + len(after)),
        out_specs=ANY,
        scratch_shapes=[
            pltpu.VMEM((slots, parts, each, tile), stored.dtype),
            pltpu.SemaphoreType.DMA((slots,)),
            pltpu.SemaphoreType.DMA((slots,)),
        ],
        compiler_params=room(56),
        cost_estimate=FREE,
    )(stored.reshape(slots, parts, each, tile), *after)


def head_block(head, bias, extra):
    width, own = head.shape
    full = pl.BlockSpec(memory_space=pltpu.VMEM)

    def kernel(head_ref, bias_ref, out_ref):
        out_ref[:own] = head_ref[...].T
        out_ref[own:] = jnp.zeros((extra, width), head.dtype)
        left = bias_ref[...]
        for part in range(width // own):
            piece = left.astype(jnp.bfloat16)
            left = left - piece.astype(jnp.float32)
            out_ref[own : own + 1, part * own : (part + 1) * own] = piece

    return pl.pallas_call(
        kernel,
        out_shape=jax.ShapeDtypeStruct((own + extra, width), head.dtype),
        in_specs=[full, full],
        out_specs=full,
        compiler_params=room(16),
        cost_estimate=FREE,
    )(head, bias[None])


def norm_pass(before, x, after, gain):
    bins, width = x.shape
    step = before.shape[0]
    full = pl.BlockSpec(memory_space=pltpu.VMEM)

    def kernel(before_ref, x_ref, after_ref, gain_ref, out_ref, xhat_ref, factor_ref, scale_ref):
        chunks = [(before_ref, 0)] + [(x_ref, i) for i in range(0, bins, step)] + [(after_ref, 0)]
        for i, (ref, top) in enumerate(chunks):
            rows = ref[pl.ds(top, step)].astype(jnp.float32)
            offset = rows - jnp.mean(rows, axis=1, keepdims=True)
            scale = lax.rsqrt(jnp.mean(offset * offset, axis=1, keepdims=True) + 1e-05)
            xhat = offset * scale
            v = xhat * gain_ref[...]
            phi = 0.5 * (1.0 + lax.erf(v * SQRT_HALF))
            out_ref[pl.ds(i * step, step)] = (v * phi).astype(jnp.bfloat16)
            if ref is x_ref:
                at = pl.ds(top, step)
                slope = phi + v * jnp.exp(-0.5 * v * v) * INV_SQRT_TAU
                xhat_ref[at] = xhat
                factor_ref[at] = slope * gain_ref[...]
                scale_ref[at] = scale

    wide = jax.ShapeDtypeStruct((bins, width), jnp.float32)
    return pl.pallas_call(
        kernel,
        out_shape=(
            jax.ShapeDtypeStruct((bins + 2 * step, width), jnp.bfloat16),
            wide,
            wide,
            jax.ShapeDtypeStruct((bins, 1), jnp.float32),
        ),
        in_specs=[full] * 4,
        out_specs=(full,) * 4,
        compiler_params=room(12),
        cost_estimate=FREE,
    )(before, x, after, gain[None])


def blank(shape, dtype):
    return pl.pallas_call(
        lambda out_ref: None,
        out_shape=jax.ShapeDtypeStruct(shape, dtype),
        out_specs=ANY,
        cost_estimate=FREE,
    )()


def pick_kernel(count, index_ref, pieces_ref, out_ref, mark_ref, sem):
    def start(i, carry):
        pltpu.make_async_copy(pieces_ref.at[index_ref[i]], out_ref.at[i], sem).start()
        return carry

    lax.fori_loop(0, count, start, 0, unroll=min(count, 8))
    mark_ref[...] = jnp.zeros_like(mark_ref)
    pltpu.make_async_copy(pieces_ref.at[pl.ds(0, count)], out_ref, sem).wait()


def pick(pieces, index):
    count = index.shape[0]
    block = (count,) + pieces.shape[1:]
    return pl.pallas_call(
        lambda *refs: pick_kernel(count, *refs),
        out_shape=(
            jax.ShapeDtypeStruct(block, pieces.dtype),
            jax.ShapeDtypeStruct((8, 128), jnp.float32),
        ),
        grid_spec=pltpu.PrefetchScalarGridSpec(
            num_scalar_prefetch=1,
            grid=(1,),
            in_specs=[ANY],
            out_specs=(
                pl.BlockSpec(block, lambda i, index: (0, 0, 0)),
                pl.BlockSpec((8, 128), lambda i, index: (0, 0)),
            ),
            scratch_shapes=[pltpu.SemaphoreType.DMA],
        ),
        compiler_params=room(16),
        cost_estimate=FREE,
    )(index, pieces)


def gate(value, *others, lead=0):
    return pl.pallas_call(
        lambda *refs: None,
        out_shape=jax.ShapeDtypeStruct(value.shape, value.dtype),
        in_specs=[ANY] * (1 + len(others)),
        out_specs=ANY,
        input_output_aliases={0: 0},
        cost_estimate=pl.CostEstimate(flops=lead * 10**9, bytes_accessed=0, transcendentals=0),
    )(value, *others)


def fetch(g, blocks, held, sems, go):
    for j, parts in enumerate(blocks):

        @pl.when(g == j)
        def _():
            top = 0
            for part in parts:
                copy = pltpu.make_async_copy(
                    part, held.at[j % 2, pl.ds(top, part.shape[0])], sems.at[j % 2]
                )
                copy.start() if go else copy.wait()
                top += part.shape[0]


def next_block(g, blocks, held, sems):
    @pl.when(g == 0)
    def _():
        fetch(g, blocks, held, sems, True)

    fetch(g, blocks, held, sems, False)
    fetch(g + 1, blocks, held, sems, True)


def nest(flat, counts):
    out = []
    for n in counts:
        out.append(flat[:n])
        flat = flat[n:]
    return out


def forward_kernel(core_ref, act_ref, x_ref, taps_ref, mix_ref, *rest):
    slope_ref, mine_ref, theirs_ref, mark_ref, embed = rest
    mark_ref[...] = jnp.zeros_like(mark_ref)
    bins = x_ref.shape[0]
    step = (act_ref.shape[0] - bins) // 2
    half = mine_ref.shape[0]

    def dot(a, b):
        return jnp.dot(a, b, preferred_element_type=jnp.float32)

    v = dot(act_ref[:bins], taps_ref[0])
    v = v + dot(act_ref[step : step + bins], taps_ref[1])
    v = v + dot(act_ref[2 * step :], taps_ref[2])
    phi = 0.5 * (1.0 + lax.erf(v * SQRT_HALF))
    slope_ref[...] = phi + v * jnp.exp(-0.5 * v * v) * INV_SQRT_TAU
    embed[...] = x_ref[...].astype(jnp.float32) + dot((v * phi).astype(jnp.bfloat16), mix_ref[...])
    at = pl.multiple_of(core_ref[0] * half, half)
    mine_ref[...] = embed[pl.ds(at, half)].astype(jnp.bfloat16)
    theirs_ref[...] = embed[pl.ds(half - at, half)].astype(jnp.bfloat16)


def forward_pass(core, act, x, taps, mix, half):
    bins, width = x.shape
    inner = taps.shape[2]
    out = jax.ShapeDtypeStruct((half, width), jnp.bfloat16)
    full = pl.BlockSpec(memory_space=pltpu.VMEM)
    return pl.pallas_call(
        forward_kernel,
        out_shape=(
            jax.ShapeDtypeStruct((bins, inner), jnp.float32),
            out,
            out,
            jax.ShapeDtypeStruct((8, 128), jnp.float32),
        ),
        in_specs=[pl.BlockSpec(memory_space=pltpu.SMEM)] + [full] * 4,
        out_specs=(full,) * 4,
        scratch_shapes=[pltpu.VMEM((bins, width), jnp.float32)],
        compiler_params=room(18),
        cost_estimate=FREE,
    )(core, act, x, taps, mix)


def head_kernel(counts, own, mine_ref, other_ref, *rest):
    sig_ref, ratio_ref, head_ref, rows, held, sems = rest[-6:]
    g = pl.program_id(0)
    half = mine_ref.shape[0]

    @pl.when(g == 0)
    def _():
        rows[:half] = mine_ref[...]
        rows[half:] = other_ref[...]

    next_block(g, nest(rest[: sum(counts)], counts), held, sems)
    w = held.at[g % 2]
    head_ref[...] = w[:own]
    logits = nt_dot(rows[...], w[:own])
    bias = jnp.sum(w[own:].astype(jnp.float32), axis=0, keepdims=True)
    for part in range(bias.shape[1] // own):
        logits = logits + bias[:, part * own : (part + 1) * own]
    e = jnp.exp(-jnp.abs(logits))
    inverse = 1.0 / (1.0 + e)
    sig = jnp.where(logits >= 0.0, inverse, e * inverse)
    pred = jnp.maximum(logits, 0.0) + jnp.log1p(e)
    sig_ref[...] = sig
    ratio_ref[...] = sig / pred


def head_pass(mine, other, blocks, own, others):
    half, width = mine.shape
    n = 2 * half
    counts = [len(parts) for parts in blocks]
    flat = [part for parts in blocks for part in parts]
    tall = blocks[0][0].shape[0]
    tracks = own * len(blocks)
    out = jax.ShapeDtypeStruct((n, tracks), jnp.float32)
    out_spec = pl.BlockSpec((n, own), lambda g: (0, g))
    row_spec = pl.BlockSpec((half, width), lambda g: (0, 0))
    return pl.pallas_call(
        lambda *refs: head_kernel(counts, own, *refs),
        out_shape=(out, out, jax.ShapeDtypeStruct((tracks, width), mine.dtype)),
        grid=(len(blocks),),
        in_specs=[row_spec, row_spec] + [ANY] * (len(flat) + len(others)),
        out_specs=(out_spec, out_spec, pl.BlockSpec((own, width), lambda g: (g, 0))),
        scratch_shapes=[
            pltpu.VMEM((n, width), jnp.bfloat16),
            pltpu.VMEM((2, tall, width), jnp.bfloat16),
            pltpu.SemaphoreType.DMA((2,)),
        ],
        compiler_params=room(14),
        cost_estimate=FREE,
    )(mine, other, *flat, *others)


def grad_kernel(kinds, own_spans, plan_ref, sig_ref, ratio_ref, *rest):
    sources = rest[:kinds]
    kept_ref, sent_ref, tiles, sems = rest[kinds:]
    half, tile = tiles.shape[1:]
    spans = sig_ref.shape[1] // tile
    per = 2 * own_spans
    usual = kinds // 2 + 1

    def copies(group, go):
        top = sum(source.shape[0] for source in sources[: group[0]])
        for k in group:
            copy = pltpu.make_async_copy(
                sources[k], tiles.at[pl.ds(top, sources[k].shape[0])], sems.at[k]
            )
            copy.start() if go else copy.wait()
            top += sources[k].shape[0]

    copies(range(usual), True)

    @pl.when(plan_ref[2 * spans] > 0)
    def _():
        copies(range(usual, kinds), True)
        copies(range(usual, kinds), False)

    copies(range(usual), False)
    for s, out_ref in enumerate((kept_ref, sent_ref)):
        for k in range(spans):
            cols = pl.ds(k * tile, tile)
            at = (pl.ds(s * half, half), cols)
            spot = plan_ref[k // own_spans * per + s * own_spans + k % own_spans]
            t = tiles[spot].astype(jnp.float32)
            out_ref[:, cols] = (sig_ref[at] - t * ratio_ref[at]).astype(jnp.bfloat16)


def grad_pass(plan, sig, ratio, sources, own_spans):
    n, tracks = sig.shape
    half, tile = sources[0].shape[1:]
    out = jax.ShapeDtypeStruct((half, tracks), jnp.bfloat16)
    full = pl.BlockSpec(memory_space=pltpu.VMEM)
    total = sum(source.shape[0] for source in sources)
    return pl.pallas_call(
        lambda *refs: grad_kernel(len(sources), own_spans, *refs),
        out_shape=(out, out),
        in_specs=[pl.BlockSpec(memory_space=pltpu.SMEM), full, full] + [ANY] * len(sources),
        out_specs=(full, full),
        scratch_shapes=[
            pltpu.VMEM((total, half, tile), jnp.bfloat16),
            pltpu.SemaphoreType.DMA((len(sources),)),
        ],
        compiler_params=room(12),
        cost_estimate=FREE,
    )(plan, sig, ratio, *sources)


def inner_pass(core, kept, back, mix, slope, step):
    half, width = kept.shape
    bins, inner = slope.shape
    full = pl.BlockSpec(memory_space=pltpu.VMEM)

    def kernel(core_ref, kept_ref, back_ref, mix_ref, slope_ref, embed_ref, pre_ref, *ends):
        at = pl.multiple_of(core_ref[0] * half, half)
        embed_ref[pl.ds(at, half)] = kept_ref[...]
        embed_ref[pl.ds(half - at, half)] = back_ref[...]
        d_inner = nt_dot(embed_ref[...].astype(jnp.bfloat16), mix_ref[...])
        d_pre = (d_inner * slope_ref[...]).astype(jnp.bfloat16)
        pre_ref[...] = d_pre
        ends[0][...] = d_pre[:step]
        ends[1][...] = d_pre[bins - step :]

    end = jax.ShapeDtypeStruct((step, inner), jnp.bfloat16)
    return pl.pallas_call(
        kernel,
        out_shape=(
            jax.ShapeDtypeStruct((bins, width), jnp.float32),
            jax.ShapeDtypeStruct((bins, inner), jnp.bfloat16),
            end,
            end,
        ),
        in_specs=[pl.BlockSpec(memory_space=pltpu.SMEM)] + [full] * 4,
        out_specs=(full,) * 4,
        compiler_params=room(10),
    )(core, kept, back, mix, slope)


def local_pass(d_pre, taps, step):
    bins = d_pre.shape[0]
    width = taps.shape[1]
    full = pl.BlockSpec(memory_space=pltpu.VMEM)

    def kernel(pre_ref, taps_ref, out_ref):
        out_ref[...] = nt_dot(pre_ref[...], taps_ref[1])
        out_ref[: bins - step] += nt_dot(pre_ref[step:], taps_ref[0])
        out_ref[step:] += nt_dot(pre_ref[: bins - step], taps_ref[2])

    return pl.pallas_call(
        kernel,
        out_shape=jax.ShapeDtypeStruct((bins, width), jnp.float32),
        in_specs=[full] * 2,
        out_specs=full,
        compiler_params=room(12),
    )(d_pre, taps)


def last_pass(before, after, d_act, taps, factor, xhat, inverse, d_embed):
    step = before.shape[0]
    bins, width = d_act.shape
    full = pl.BlockSpec(memory_space=pltpu.VMEM)

    def kernel(before_ref, after_ref, act_ref, first_ref, last_ref, *rest):
        factor_ref, xhat_ref, inverse_ref, embed_ref, out_ref = rest
        head = nt_dot(before_ref[...], last_ref[0])
        tail = nt_dot(after_ref[...], first_ref[0])
        for top in range(0, bins, step):
            at = pl.ds(top, step)
            d = act_ref[at]
            if top == 0:
                d = d + head
            if top == bins - step:
                d = d + tail
            d = d * factor_ref[at]
            xhat = xhat_ref[at]
            middle = jnp.mean(d, axis=1, keepdims=True)
            slant = jnp.mean(d * xhat, axis=1, keepdims=True)
            out_ref[at] = embed_ref[at] + inverse_ref[at] * (d - middle - xhat * slant)

    def tap(i):
        return pl.BlockSpec((1,) + taps.shape[1:], lambda j: (i, 0, 0))

    return pl.pallas_call(
        kernel,
        out_shape=jax.ShapeDtypeStruct((bins, width), jnp.float32),
        grid=(1,),
        in_specs=[full] * 3 + [tap(0), tap(2)] + [full] * 4,
        out_specs=full,
        compiler_params=room(16),
    )(before, after, d_act, taps, taps, factor, xhat, inverse, d_embed)


def shards(
    inputs,
    layernorm_gain,
    dilated_weight,
    mix_weight,
    head_weight,
    head_bias,
    stored_tiles,
    slot_tiles,
):
    n_q = lax.axis_size(SEQ)
    n_x = lax.axis_size("x")
    n_c = lax.axis_size("core")
    x_index = lax.axis_index("x")
    core = lax.axis_index("core")
    bins, width = inputs.shape[1:]
    half = bins // n_c
    tracks = head_weight.shape[1] * n_x * n_c
    slots, _, tile = stored_tiles.shape
    spans = tracks // tile
    depth = n_q * n_c * slots
    want = n_c * spans
    own_tracks = head_weight.shape[1]
    own_spans = own_tracks // tile

    def step(value, shift):
        return lax.ppermute(value, "x", [(i, (i + shift) % n_x) for i in range(n_x)])

    before, after = halo(inputs[0, bins - DILATION_STEP :], inputs[0, :DILATION_STEP])
    block = head_block(head_weight, head_bias, 16)
    outbound = gate(arrange(stored_tiles, n_q * n_c, (block,)), before, after)
    pieces = lax.all_to_all(
        outbound.reshape(depth, half, tile), ("z", "y", "core"), 0, 0, tiled=True
    )
    near = [step(block, 1), step(block, -1)]
    block_x = (x_index + jnp.array([0, 0, -1, -1, 1, 1, 2, 2], jnp.int32)) % n_x
    block_c = (core + jnp.array([0, 1, 0, 1, 0, 1, 0, 1], jnp.int32)) % n_c
    group_of = block_x * n_c + block_c

    table = slot_tiles.reshape(n_q, n_x, n_c * slots).transpose(1, 0, 2).reshape(n_x, depth)
    dest = jnp.where(table >= 0, table // want, n_x)
    chips = jnp.arange(n_x, dtype=jnp.int32)
    marks = dest[:, :, None] == chips[None, None, :]
    place = jnp.arange(depth, dtype=jnp.int32)
    same = dest[:, :, None] == dest[:, None, :]
    rank = jnp.sum(same & (place[None, None, :] < place[None, :, None]), axis=2, dtype=jnp.int32)
    sizes = jnp.sum(marks, axis=1, dtype=jnp.int32)
    fullest = jnp.max(jnp.where(chips[:, None] == chips[None, :], 0, sizes))
    my_dest = lax.dynamic_index_in_dim(dest, x_index, 0, keepdims=False)
    my_rank = lax.dynamic_index_in_dim(rank, x_index, 0, keepdims=False)
    shifted = (my_dest - x_index) % n_x
    shifted = jnp.where(my_dest < n_x, shifted, n_x)
    order = jnp.arange(want, dtype=jnp.int32)
    hit = (shifted[None, None, :] == chips[:, None, None]) & (
        my_rank[None, None, :] == order[None, :, None]
    )
    outgoing = jnp.sum(hit * place, axis=2, dtype=jnp.int32)

    spots = jnp.arange(want, dtype=jnp.int32)
    spot_side = spots // own_spans % n_c
    spot_span = (
        jnp.repeat(group_of, n_c * own_spans, total_repeat_length=want) * own_spans
        + spots % own_spans
    )
    tiles_wanted = (x_index * n_c + (core + spot_side) % n_c) * spans + spot_span
    turn = ((x_index - chips) % n_x)[:, None]
    spill = want - ROOM
    usual = want + (turn - 1) * ROOM + rank
    rare = want + (n_x - 1) * ROOM + (turn - 1) * spill + rank - ROOM
    spot_in = jnp.where(turn == 0, rank, jnp.where(rank < ROOM, usual, rare))
    found = tiles_wanted[:, None, None] == table[None]
    plan = jnp.sum(found * spot_in[None], axis=(1, 2), dtype=jnp.int32)
    plan = jnp.concatenate([plan, (fullest > ROOM).astype(jnp.int32)[None]])

    core_at = core.astype(jnp.int32)[None]
    act, xhat, factor, scale = norm_pass(before, inputs[0], after, layernorm_gain)
    cut = own_tracks // 2
    far = [
        step(gate(near[0][:cut], plan, scale), 1),
        step(gate(near[1][cut:], plan, scale), -1),
    ]
    slope, mine, theirs, mark = forward_pass(
        core_at, act, inputs[0], dilated_weight, mix_weight, half
    )
    blocks = []
    for parts in ([block], [near[0]], [near[1]]):
        blocks += [parts, [core_swap(part) for part in parts]]
    blocks += [far, [core_swap(gate(part, mark)) for part in far]]
    other = core_swap(theirs)

    outgoing = gate(outgoing, plan, other, *blocks[-1], lead=LEAD)
    picked = {d: pick(pieces, outgoing[d, :ROOM])[0] for d in (2, 1, 3)}
    sent = {d: step(picked[d], d) for d in (2, 1, 3)}
    arrived = [sent[d] for d in range(1, n_x)]

    def extra(first, last):
        def send(pieces, outgoing):
            out = []
            for d in range(1, n_x):
                v = step(pick(pieces, outgoing[d, first:last])[0], d)
                out.append(jnp.pad(v, ((0, want - last), (0, 0), (0, 0))))
            return tuple(out)

        return send

    def roomy(pieces, outgoing):
        shape = (want - ROOM,) + pieces.shape[1:]
        return tuple(blank(shape, pieces.dtype) for _ in range(n_x - 1))

    level = (fullest > ROOM).astype(jnp.int32) + (fullest > ROOM + SPARE)
    more = lax.switch(
        level,
        [roomy, extra(ROOM, ROOM + SPARE), extra(ROOM, want)],
        pieces,
        outgoing,
    )
    local, _ = pick(pieces, outgoing[0])
    sig, ratio, full_head = head_pass(mine, other, blocks, own_tracks, [local] + list(more))
    d_mine, d_theirs = grad_pass(plan, sig, ratio, [local] + arrived + list(more), own_spans)
    leaving = jnp.dot(d_theirs, full_head, preferred_element_type=jnp.float32)
    kept = jnp.dot(d_mine, full_head, preferred_element_type=jnp.float32)
    d_embed, d_pre, first, last = inner_pass(
        core_at, kept, core_swap(leaving), mix_weight, slope, DILATION_STEP
    )
    before, after = halo(last, first)
    d_act = local_pass(d_pre, dilated_weight, DILATION_STEP)
    grad = last_pass(before, after, d_act, dilated_weight, factor, xhat, scale, d_embed)
    return grad[None]


def solution(mesh):
    chips = jax.sharding.Mesh(
        np.asarray(mesh.devices).reshape(4, 4, 4, 2), ("z", "y", "x", "core")
    )
    in_specs = (
        P(TRK, SEQ, None),
        P(),
        P(),
        P(),
        P(None, TRK),
        P(TRK),
        P(SEQ + TRK, None, None),
        P(),
    )
    out_specs = P(TRK, SEQ, None)
    return jax.shard_map(
        shards, mesh=chips, in_specs=in_specs, out_specs=out_specs, check_vma=False
    )
```
